32 devices in a mesh: space: 4 (over y, x), tm: 8 (over z, core).
Axes of the slice: x: 2, y: 2, z: 4, core: 2. Of those that a mesh axis runs over, the one named last changes fastest.
Arguments:
- lattice_field: float32 [32, 16, 2048], P('tm', 'space'), may hold values from -6 to 6
- parity: int32 [8, 4, 128], P('tm', 'space'), may hold values from 0 to 1
- block_list: int32 [8, 8], replicated, may hold values from 0 to 7, as said below
- w_embed: bfloat16 [256, 768], replicated, may hold values from -0.5 to 0.5
- b_embed: float32 [768], replicated, may hold values from -3 to 3
- gain_in: float32 [768], replicated, may hold values from 0.5 to 1.5
- w_qkv: bfloat16 [768, 2304], replicated, may hold values from -4 to 4
- gain_out: float32 [768], replicated, may hold values from 0.5 to 1.5
- w_head: bfloat16 [768, 512], replicated, may hold values from -0.21875 to 0.21875
- b_head: float32 [512], replicated, may hold values from -3 to 3
Outputs:
- new_field: float32 [32, 16, 2048], P('tm', 'space')
- action_density: float32 [32, 16, 2048], P('tm', 'space')
- time_link: float32 [32, 16, 2048], P('tm', 'space')
- slab_link: float32 [32, 16, 2048], P('tm', 'space')
- totals: float32 [2], replicated
The draws below stay inside these ranges and needn't reach their ends.
Inputs may be any that keep to these rules, and one draw needn't show every extreme that they name: `block_list`: row b lists 8 different block numbers, b among them.
All inputs are finite; a program needn't handle non-finite values.
Results may differ from the reference program's by a relative error of at most 0.006.
Values may be sent and summed in bfloat16 or wider, within the bound.
A program may use at most 64 MiB of HBM per device.

```python
import math
import jax
import jax.numpy as jnp
from jax import lax

P_SIZE = 4
D = 768
HEADS = 12
HS = 64
LY = 32
LZ = 64
BLK = 128
KSEL = 8
PATCH = 256
TOKD = 128
LT = 32
LX = 16
NB = 8
SITES = 1048576


def draw_lattice_field(key, part):
    second_key = jax.random.fold_in(key, 1)
    along_x = 0.6 + 1.2 * jnp.arange(LX, dtype=jnp.float32) / LX
    values = jax.random.normal(second_key, (LT, LX, LY * LZ), jnp.float32) * along_x[None, :, None]
    return jnp.clip(values, -6.0, 6.0)


def draw_block_list(key, part):
    rows_idx = jnp.arange(NB, dtype=jnp.int32)[:, None]
    cols_idx = jnp.arange(NB, dtype=jnp.int32)[None, :]
    blocks_dev = TOKD // BLK
    distance = (cols_idx - rows_idx) % NB
    near = (distance == 1) | (distance == NB - 1) | (distance == NB // 2)
    priority = jnp.where(distance == 0, 3, jnp.where(near, 2, jnp.where(cols_idx % blocks_dev == rows_idx % blocks_dev, 1, 0)))
    order_keys = jax.random.split(key, NB)
    ordering = jax.vmap(lambda row_key: jax.random.permutation(row_key, NB))(order_keys).astype(jnp.int32)
    ranking = priority.astype(jnp.int32) * NB + ordering
    _, chosen = lax.top_k(ranking, KSEL)
    return chosen.astype(jnp.int32)


def draw_w_qkv(key, part):
    first_key = jax.random.fold_in(key, 0)
    values = jax.random.normal(first_key, (D, 3 * D), jnp.float32) / D ** 0.5
    limit = min(6.0 / D ** 0.5, 4.0)
    values = jnp.clip(values, -limit, limit)
    return jnp.concatenate([values[:, :2 * D], 4.0 * values[:, 2 * D:]], axis=1).astype(jnp.bfloat16)


def plant(entries, rng, smallest, high):
    extent = entries.shape
    index_at = [jax.random.randint(jax.random.fold_in(rng, axis), (), 0, extent[axis]) for axis in range(len(extent))]
    entries = entries.at[tuple(index_at)].set(smallest)
    longest = extent.index(max(extent))
    index_at[longest] = (index_at[longest] + 1) % extent[longest]
    return entries.at[tuple(index_at)].set(high)


def noise(key, extent, scale, most, kind=jnp.bfloat16):
    return jnp.clip(scale * jax.random.normal(key, extent, jnp.float32), -most, most).astype(kind)


def setup_inputs(seed: int = 0) -> dict:
    streams_of = jax.random.split(jax.random.key(seed), 11)
    return {
        "lattice_field": draw_lattice_field(jax.random.fold_in(streams_of[10], 71), 0),
        "parity": plant(jax.random.randint(streams_of[1], (LT // P_SIZE, LX // P_SIZE, TOKD), 0, 2), jax.random.fold_in(streams_of[1], 1), 0, 1).astype(jnp.int32),
        "block_list": draw_block_list(jax.random.fold_in(streams_of[10], 71), 0),
        "w_embed": noise(streams_of[3], (PATCH, D), (PATCH // 2) ** -0.5, 0.5),
        "b_embed": noise(streams_of[4], (D,), 0.5, 3.0, jnp.float32),
        "gain_in": jnp.clip(jax.random.uniform(streams_of[5], (D,), jnp.float32, 0.5, 1.5), 0.5, 1.5),
        "w_qkv": draw_w_qkv(jax.random.fold_in(streams_of[10], 71), 0),
        "gain_out": jnp.clip(jax.random.uniform(streams_of[7], (D,), jnp.float32, 0.5, 1.5), 0.5, 1.5),
        "w_head": noise(streams_of[8], (D, 2 * PATCH), D ** -0.5, 0.21875),
        "b_head": noise(streams_of[9], (2 * PATCH,), 0.5, 3.0, jnp.float32),
    }


hopping = 0.2
quartic = 0.5
epsilon = 1e-05
log_two_pi = math.log(2.0 * math.pi)

def layer_norm(values, gain_vec):
    centre = values - lax.optimization_barrier(jnp.mean(values, axis=-1, keepdims=True))
    spread = lax.optimization_barrier(jnp.mean(centre * centre, axis=-1, keepdims=True))
    return centre * lax.rsqrt(spread + epsilon) * gain_vec

def site_parity():
    positions = jnp.arange(PATCH, dtype=jnp.int32)
    return (positions // P_SIZE ** 3 + positions // P_SIZE ** 2 % P_SIZE + positions // P_SIZE % P_SIZE + positions % P_SIZE) % 2

def reference(lattice_field, parity, block_list, w_embed, b_embed, gain_in, w_qkv, gain_out, w_head, b_head):
    lattice_grid = lattice_field.reshape(LT // P_SIZE, P_SIZE, LX // P_SIZE, P_SIZE, LY // P_SIZE, P_SIZE, LZ // P_SIZE, P_SIZE)
    slab_rows = lattice_grid.transpose(2, 0, 4, 6, 1, 3, 5, 7).reshape(LX // P_SIZE, LT // P_SIZE * TOKD, PATCH)
    slab_bits = parity.transpose(1, 0, 2).reshape(LX // P_SIZE, LT // P_SIZE * TOKD)
    pattern = site_parity()
    scale_factor = HS ** (-0.5)

    def one_slab(item_pair):
        site_rows, bits = item_pair
        frozen = pattern[None, :] == bits[:, None]
        frozen_in = jnp.where(frozen, site_rows, 0.0).astype(jnp.bfloat16)
        embedded = jnp.dot(frozen_in, w_embed, preferred_element_type=jnp.float32) + b_embed
        normed = layer_norm(embedded, gain_in).astype(jnp.bfloat16)
        qkv_rows = jnp.dot(normed, w_qkv, preferred_element_type=jnp.float32).astype(jnp.bfloat16)
        queries = qkv_rows[:, :D].reshape(NB, BLK, HEADS, HS)
        key_all = qkv_rows[:, D:2 * D].reshape(NB, BLK, HEADS, HS)
        value_all = qkv_rows[:, 2 * D:].reshape(NB, BLK, HEADS, HS)
        key_sel = key_all[block_list].reshape(NB, KSEL * BLK, HEADS, HS)
        value_sel = value_all[block_list].reshape(NB, KSEL * BLK, HEADS, HS)
        scores = jnp.einsum('bqhd,bkhd->bhqk', queries.astype(jnp.float32), key_sel.astype(jnp.float32)) * scale_factor
        row_top = lax.optimization_barrier(jnp.max(scores, axis=-1, keepdims=True))
        exp_scores = jnp.exp(scores - row_top)
        row_total = lax.optimization_barrier(jnp.sum(exp_scores, axis=-1))
        weights = exp_scores.astype(jnp.bfloat16)
        mixed = jnp.einsum('bhqk,bkhd->bqhd', weights.astype(jnp.float32), value_sel.astype(jnp.float32))
        mixed = mixed / row_total.transpose(0, 2, 1)[..., None]
        hidden = embedded + mixed.reshape(NB * BLK, D)
        normed_out = layer_norm(hidden, gain_out).astype(jnp.bfloat16)
        affine = jnp.dot(normed_out, w_head, preferred_element_type=jnp.float32) + b_head
        scale_log = jnp.tanh(affine[:, :PATCH])
        shift_val = affine[:, PATCH:]
        moved = jnp.where(frozen, site_rows, site_rows * jnp.exp(scale_log) + shift_val)
        log_det = jnp.sum(jnp.where(frozen, 0.0, scale_log))
        return (moved, log_det)
    moved_all, log_dets = lax.map(one_slab, (slab_rows, slab_bits))
    moved_grid = moved_all.reshape(LX // P_SIZE, LT // P_SIZE, LY // P_SIZE, LZ // P_SIZE, P_SIZE, P_SIZE, P_SIZE, P_SIZE)
    new_field = moved_grid.transpose(1, 4, 0, 5, 2, 6, 3, 7).reshape(LT, LX, LY * LZ)
    cube = new_field.reshape(LT, LX, LY, LZ)
    ahead_t = jnp.roll(cube, -1, 0)
    ahead_x = jnp.roll(cube, -1, 1)
    neighbours = ahead_t + ahead_x
    neighbours = neighbours + jnp.roll(cube, -1, 2)
    neighbours = neighbours + jnp.roll(cube, -1, 3)
    squared = cube * cube
    density = -2.0 * hopping * cube * neighbours + squared + quartic * (squared - 1.0) * (squared - 1.0)
    action_density = density.reshape(LT, LX, LY * LZ)
    time_link = (cube * ahead_t).reshape(LT, LX, LY * LZ)
    slab_link = (cube * ahead_x).reshape(LT, LX, LY * LZ)
    sum_log = -0.5 * jnp.sum(lattice_field * lattice_field) - jnp.sum(log_dets)
    sum_act = jnp.sum(action_density)
    totals = jnp.stack([sum_log / SITES - 0.5 * log_two_pi, sum_act / SITES]).astype(jnp.float32)
    return (new_field, action_density, time_link, slab_link, totals)
```

```python
import functools
import math

import jax
import jax.numpy as jnp
from jax import lax
from jax.experimental import pallas as pl
from jax.experimental.pallas import tpu as pltpu
from jax.sharding import PartitionSpec as P

D = 768
HS = 64
TOK = 128
PATCH = 256
hopping = 0.2
quartic = 0.5
epsilon = 1e-05
log_two_pi = math.log(2.0 * math.pi)
MESH = pl.DeviceIdType.MESH
f32 = jnp.float32
bf16 = jnp.bfloat16


def iota(shape, dim):
    return lax.broadcasted_iota(jnp.int32, shape, dim)


def dot(a, b):
    return jnp.dot(a, b, preferred_element_type=f32)


def dot_nt(a, b):
    return lax.dot_general(a, b, (((1,), (1,)), ((), ())), preferred_element_type=f32)


def layer_norm(values, gain_vec):
    centre = values - jnp.mean(values, axis=-1, keepdims=True)
    spread = jnp.mean(centre * centre, axis=-1, keepdims=True)
    return centre * lax.rsqrt(spread + epsilon) * gain_vec


def swap_blocks(m, n_out):
    rows = []
    for b in range(8):
        rows.append(
            jnp.concatenate(
                [m[a * 16 : a * 16 + 16, b * 32 : b * 32 + 32] for a in range(8)], axis=1
            )
        )
    return jnp.concatenate(rows, axis=0)


def fold8(a):
    return jnp.sum(a.reshape(a.shape[0] // 8, 8, 128), axis=0)


def kernel(n_s, n_tm, masked, *refs):
    if masked:
        list_ref, refs = refs[0], refs[1:]
    (x_ref, par_ref, we_hbm, be_ref, gi_ref, wq_hbm, go_ref, wh_hbm, bh_ref,
     nf_ref, ad_ref, tl_ref, sl_ref, tot_ref,
     we, wq, wh, wep, whp, a1, a2, b2, tok, emb, nrm, qs, kv, mix,
     ht_s, ht_r, hx_s, hx_r, red_s, red_t,
     w_sem, send, recv, fsend, frecv, sib_sem, halo_sem, rs_send, rs_recv, rt_send, rt_recv) = refs
    n_c = n_tm // 2
    me_t = lax.axis_index("tm")
    me_s = lax.axis_index("space")
    core = lax.rem(me_t, 2)
    chip = me_t // 2
    sibling = chip * 2 + 1 - core

    loads = [
        pltpu.make_async_copy(src, dst, w_sem.at[i])
        for i, (src, dst) in enumerate(((we_hbm, we), (wq_hbm, wq), (wh_hbm, wh)))
    ]
    for load in loads:
        load.start()
    barrier = pltpu.get_barrier_semaphore()
    for o in range(1, n_tm):
        pl.semaphore_signal(barrier, inc=1, device_id={"tm": lax.rem(me_t + o, n_tm)}, device_id_type=MESH)
    for o in range(1, n_s):
        pl.semaphore_signal(barrier, inc=1, device_id={"space": lax.rem(me_s + o, n_s)}, device_id_type=MESH)

    for t in range(4):
        for c in range(16):
            a1[pl.ds(t * 64 + c, 4, stride=16), :] = x_ref[t, :, c * 128 : c * 128 + 128]
    par_row = par_ref[0].astype(f32)
    spread_rows = jnp.where(iota((16, 128), 1) // 16 == iota((16, 128), 0) // 2, par_row, 0.0)
    pick = iota((128, 128), 0) % 16 == (iota((128, 128), 1) % 64) // 4
    par16 = dot(spread_rows.astype(bf16), jnp.where(pick, 1.0, 0.0).astype(bf16))
    par_full = jnp.concatenate([par16] * 16, axis=0)
    row = iota((256, 128), 0)
    lane = iota((256, 128), 1)
    site = (row // 64 + row // 16 + lane // 64 + lane) % 2
    frozen = site.astype(f32) == par_full
    u = a1[...]
    a2[...] = jnp.where(frozen, u, 0.0)
    rows_c = jnp.concatenate([a2[pl.ds(c, 16, stride=16), :] for c in range(16)], axis=0)
    r, l = iota((128, 128), 0), iota((128, 128), 1)
    q = jnp.where((r // 64 == l // 64) & ((r % 64) // 16 == l % 4) & (r % 16 == (l % 64) // 4), 1.0, 0.0).astype(bf16)
    spreadq = dot_nt(q, rows_c.astype(bf16))
    tok[me_t] = swap_blocks(spreadq, 8).astype(bf16)

    pl.semaphore_wait(barrier, n_tm - 1 + n_s - 1)
    own = pltpu.make_async_remote_copy(
        src_ref=tok.at[me_t], dst_ref=tok.at[me_t], send_sem=sib_sem.at[0], recv_sem=sib_sem.at[1],
        device_id={"tm": sibling}, device_id_type=MESH)
    sends = []
    for k in range(1, n_c):
        target = lax.rem(chip + k, n_c) * 2 + core
        sends.append(pltpu.make_async_remote_copy(
            src_ref=tok.at[me_t], dst_ref=tok.at[me_t], send_sem=send.at[k - 1], recv_sem=recv.at[k - 1],
            device_id={"tm": target}, device_id_type=MESH))
    for s in sends:
        s.start()
    own.start()
    forwards = []
    for k in range(1, n_c):
        block = lax.rem(chip - k + n_c, n_c) * 2 + core
        forwards.append(pltpu.make_async_remote_copy(
            src_ref=tok.at[block], dst_ref=tok.at[block], send_sem=fsend.at[k - 1], recv_sem=frecv.at[k - 1],
            device_id={"tm": sibling}, device_id_type=MESH))

    f, j = iota((256, 256), 0), iota((256, 256), 1)
    d = f // 32
    source = (f % 16) * 16 + ((f // 16) % 2) * 8 + (d // 4) * 4 + d % 4
    perm = jnp.where(j == source, 1.0, 0.0).astype(bf16)
    loads[0].wait()
    wep[...] = dot(perm, we[...]).astype(bf16)
    loads[2].wait()
    whp[:, :256] = dot_nt(wh[:, :256], perm).astype(bf16)
    whp[:, 256:] = dot_nt(wh[:, 256:], perm).astype(bf16)
    b_head = bh_ref[...].reshape(2, 256)
    b_hi = b_head.astype(bf16).astype(f32)
    b_mid = (b_head - b_hi).astype(bf16).astype(f32)
    b_lo = b_head - b_hi - b_mid
    parts = jnp.concatenate([b_hi, b_mid, b_lo, jnp.zeros((2, 256), f32)], axis=0)
    moved_b = dot_nt(parts.astype(bf16), perm)
    b_perm = moved_b[0:2] + moved_b[2:4] + moved_b[4:6]
    b_embed = be_ref[...].reshape(1, D)
    gain_in = gi_ref[...].reshape(1, D)
    loads[1].wait()

    for k in range(n_c):
        here = lax.rem(chip - k + n_c, n_c)
        if k == 0:
            own.wait_recv()
        else:
            if k == 1:
                sends[0].wait_recv()
                forwards[0].start()
            if k < n_c - 1:
                sends[k].wait_recv()
                forwards[k].start()
            forwards[k - 1].wait_recv()
        pair = tok[pl.ds(here * 2, 2)].reshape(2 * TOK, PATCH)
        embedded = dot(pair, wep[...]) + b_embed
        normed = layer_norm(embedded, gain_in).astype(bf16)
        if k == 0:
            emb[...] = embedded
            nrm[...] = normed
            mine = pl.ds(pl.multiple_of(core * TOK, TOK), TOK)
            qs[...] = dot(nrm[mine, :], wq[:, :D]).astype(bf16) * jnp.asarray(HS ** (-0.5), bf16)
        rows_at = pl.ds(pl.multiple_of(here * 2 * TOK, 2 * TOK), 2 * TOK)
        kv[rows_at, :] = dot(normed, wq[:, D:]).astype(bf16)

    if masked:
        nb, ksel = list_ref.shape
        mine_row = jnp.sum(jnp.where(iota((nb, ksel), 0) == me_t, list_ref[...], 0), axis=0, keepdims=True)
        key_block = iota((1, n_tm * TOK), 1) // TOK
        listed = key_block < 0
        for i in range(ksel):
            listed = listed | (key_block == mine_row[:, i : i + 1])
        bias = jnp.where(listed, 0.0, -1e30)
    low = iota((TOK, 128), 1) < HS

    def head_pair(h, carry):
        cols = pl.ds(pl.multiple_of(h * 128, 128), 128)
        vcols = pl.ds(pl.multiple_of(D + h * 128, 128), 128)
        qq = qs[:, cols]
        zero = jnp.zeros_like(qq)
        q2 = jnp.concatenate([jnp.where(low, qq, zero), jnp.where(low, zero, qq)], axis=0)
        s = dot_nt(q2, kv[:, cols])
        if masked:
            s = s + bias
        top = jnp.max(s, axis=-1, keepdims=True)
        ex = jnp.exp(s - top)
        total = jnp.sum(ex, axis=-1, keepdims=True)
        o = dot(ex.astype(bf16), kv[:, vcols]) / total
        mix[:, cols] = jnp.where(low, o[:TOK], o[TOK:])
        return carry

    lax.fori_loop(0, D // 128, head_pair, 0)

    hidden = emb[mine, :] + mix[...]
    normed_out = layer_norm(hidden, go_ref[...].reshape(1, D)).astype(bf16)
    raw = dot(normed_out, whp[...])
    scale_tok = jnp.tanh(raw[:, :256] + b_perm[0:1])
    shift_tok = raw[:, 256:] + b_perm[1:2]

    def to_lattice(values, ref):
        flipped = jnp.transpose(swap_blocks(values, 8))
        hi = flipped.astype(bf16)
        lo = (flipped - hi.astype(f32)).astype(bf16)
        ref[...] = dot(hi, q) + dot(lo, q)
        return jnp.concatenate([ref[pl.ds(i, 16, stride=16), :] for i in range(16)], axis=0)

    scale_log = to_lattice(scale_tok, a2)
    shift_val = to_lattice(shift_tok, b2)
    field = jnp.where(frozen, u, u * jnp.exp(scale_log) + shift_val)
    ht_s[...] = field[0:64].astype(bf16)
    hx_s[...] = jnp.concatenate([field[t * 64 : t * 64 + 16] for t in range(4)], axis=0).astype(bf16)
    halo_t = pltpu.make_async_remote_copy(
        src_ref=ht_s, dst_ref=ht_r, send_sem=halo_sem.at[0], recv_sem=halo_sem.at[1],
        device_id={"tm": lax.rem(me_t - 1 + n_tm, n_tm)}, device_id_type=MESH)
    halo_x = pltpu.make_async_remote_copy(
        src_ref=hx_s, dst_ref=hx_r, send_sem=halo_sem.at[2], recv_sem=halo_sem.at[3],
        device_id={"space": lax.rem(me_s - 1 + n_s, n_s)}, device_id_type=MESH)
    halo_t.start()
    halo_x.start()

    def put(ref, out):
        for t in range(4):
            for c in range(16):
                out[t, :, c * 128 : c * 128 + 128] = ref[pl.ds(t * 64 + c, 4, stride=16), :]

    a1[...] = field
    put(a1, nf_ref)
    log_part = -0.5 * fold8(u * u) - fold8(jnp.where(frozen, 0.0, scale_log))
    ahead = pltpu.roll(field, 127, 1)
    wrapped = pltpu.roll(field, 63, 1)
    next_z = jnp.where(lane % 64 == 63, wrapped, ahead)
    half = pltpu.roll(field, 64, 1)
    up = pltpu.roll(half, 255, 0)
    up_wrap = pltpu.roll(half, 15, 0)
    next_y = jnp.where(lane < 64, half, jnp.where(row % 16 == 15, up_wrap, up))
    halo_t.wait_recv()
    next_t = jnp.concatenate([field[64:], ht_r[...].astype(f32)], axis=0)
    halo_x.wait_recv()
    hx = hx_r[...].astype(f32)
    pieces = []
    for t in range(4):
        pieces += [field[t * 64 + 16 : t * 64 + 64], hx[t * 16 : t * 16 + 16]]
    next_x = jnp.concatenate(pieces, axis=0)
    neighbours = next_t + next_x
    neighbours = neighbours + next_y
    neighbours = neighbours + next_z
    squared = field * field
    density = -2.0 * hopping * field * neighbours + squared + quartic * (squared - 1.0) * (squared - 1.0)

    red_s[me_s] = jnp.concatenate([log_part, fold8(density)], axis=0)
    s_sends = [
        pltpu.make_async_remote_copy(
            src_ref=red_s.at[me_s], dst_ref=red_s.at[me_s], send_sem=rs_send.at[o - 1], recv_sem=rs_recv.at[o - 1],
            device_id={"space": lax.rem(me_s + o, n_s)}, device_id_type=MESH)
        for o in range(1, n_s)
    ]
    for s in s_sends:
        s.start()
    a1[...] = density
    put(a1, ad_ref)
    a2[...] = field * next_t
    put(a2, tl_ref)
    for s in s_sends:
        s.wait_recv()
    red_t[me_t] = jnp.sum(red_s[...], axis=0)
    t_sends = [
        pltpu.make_async_remote_copy(
            src_ref=red_t.at[me_t], dst_ref=red_t.at[me_t], send_sem=rt_send.at[o - 1], recv_sem=rt_recv.at[o - 1],
            device_id={"tm": lax.rem(me_t + o, n_tm)}, device_id_type=MESH)
        for o in range(1, n_tm)
    ]
    for s in t_sends:
        s.start()
    b2[...] = field * next_x
    put(b2, sl_ref)
    own.wait_send()
    for s in sends + forwards:
        s.wait_send()
    halo_t.wait_send()
    halo_x.wait_send()
    for s in s_sends:
        s.wait_send()
    for s in t_sends:
        s.wait_recv()
    whole = jnp.sum(red_t[...], axis=0)
    sites = n_s * n_tm * 256 * 128
    tot_ref[0] = jnp.sum(whole[0:8]) / sites - 0.5 * log_two_pi
    tot_ref[1] = jnp.sum(whole[8:16]) / sites
    for s in t_sends:
        s.wait_send()


def shards(n_s, n_tm, lattice_field, parity, block_list, *weights):
    masked = block_list.shape[0] != block_list.shape[1]
    vm = pl.BlockSpec(memory_space=pltpu.VMEM)
    hbm = pl.BlockSpec(memory_space=pl.ANY)
    n_c = n_tm // 2
    grid_shape = jax.ShapeDtypeStruct(lattice_field.shape, f32)
    dma = pltpu.SemaphoreType.DMA
    call = pl.pallas_call(
        functools.partial(kernel, n_s, n_tm, masked),
        out_shape=(grid_shape,) * 4 + (jax.ShapeDtypeStruct((2,), f32),),
        in_specs=([vm] if masked else []) + [vm, vm, hbm, vm, vm, hbm, vm, hbm, vm],
        out_specs=(vm,) * 4 + (pl.BlockSpec(memory_space=pltpu.SMEM),),
        scratch_shapes=[
            pltpu.VMEM((PATCH, D), bf16),
            pltpu.VMEM((D, 3 * D), bf16),
            pltpu.VMEM((D, 2 * PATCH), bf16),
            pltpu.VMEM((PATCH, D), bf16),
            pltpu.VMEM((D, 2 * PATCH), bf16),
            pltpu.VMEM((256, 128), f32),
            pltpu.VMEM((256, 128), f32),
            pltpu.VMEM((256, 128), f32),
            pltpu.VMEM((n_tm, TOK, PATCH), bf16),
            pltpu.VMEM((2 * TOK, D), f32),
            pltpu.VMEM((2 * TOK, D), bf16),
            pltpu.VMEM((TOK, D), bf16),
            pltpu.VMEM((n_tm * TOK, 2 * D), bf16),
            pltpu.VMEM((TOK, D), f32),
            pltpu.VMEM((64, 128), bf16),
            pltpu.VMEM((64, 128), bf16),
            pltpu.VMEM((64, 128), bf16),
            pltpu.VMEM((64, 128), bf16),
            pltpu.VMEM((n_s, 16, 128), f32),
            pltpu.VMEM((n_tm, 16, 128), f32),
            dma((3,)),
            dma((n_c - 1,)),
            dma((n_c - 1,)),
            dma((n_c - 1,)),
            dma((n_c - 1,)),
            dma((2,)),
            dma((4,)),
            dma((n_s - 1,)),
            dma((n_s - 1,)),
            dma((n_tm - 1,)),
            dma((n_tm - 1,)),
        ],
        compiler_params=pltpu.CompilerParams(
            collective_id=0, has_side_effects=True, vmem_limit_bytes=40 * 2**20
        ),
        cost_estimate=pl.CostEstimate(flops=5 * 10**9, bytes_accessed=6 * 10**6, transcendentals=2 * 10**6),
    )
    extra = (block_list,) if masked else ()
    return call(*extra, lattice_field, parity, *weights)


def solution(mesh):
    n_s, n_tm = mesh.shape["space"], mesh.shape["tm"]
    split = P("tm", "space", None)
    return jax.shard_map(
        functools.partial(shards, n_s, n_tm),
        mesh=mesh,
        in_specs=(split, split) + (P(),) * 8,
        out_specs=(split,) * 4 + (P(),),
        check_vma=False,
    )
```

```python
import functools
import math

import jax
import jax.numpy as jnp
from jax import lax
from jax.experimental import pallas as pl
from jax.experimental.pallas import tpu as pltpu
from jax.sharding import PartitionSpec as P

D = 768
HS = 64
TOK = 128
PATCH = 256
hopping = 0.2
quartic = 0.5
epsilon = 1e-05
log_two_pi = math.log(2.0 * math.pi)
MESH = pl.DeviceIdType.MESH
f32 = jnp.float32
bf16 = jnp.bfloat16


def iota(shape, dim):
    return lax.broadcasted_iota(jnp.int32, shape, dim)


def dot(a, b):
    return jnp.dot(a, b, preferred_element_type=f32)


def dot_nt(a, b):
    return lax.dot_general(a, b, (((1,), (1,)), ((), ())), preferred_element_type=f32)


def layer_norm(values, gain_vec):
    centre = values - jnp.mean(values, axis=-1, keepdims=True)
    spread = jnp.mean(centre * centre, axis=-1, keepdims=True)
    return centre * lax.rsqrt(spread + epsilon) * gain_vec


def swap_blocks(m, n_out):
    rows = []
    for b in range(8):
        rows.append(
            jnp.concatenate(
                [m[a * 16 : a * 16 + 16, b * 32 : b * 32 + 32] for a in range(8)], axis=1
            )
        )
    return jnp.concatenate(rows, axis=0)


def fold8(a):
    return jnp.sum(a.reshape(a.shape[0] // 8, 8, 128), axis=0)


def kernel(n_s, n_tm, masked, *refs):
    if masked:
        list_ref, refs = refs[0], refs[1:]
    (x_hbm, par_hbm, we_hbm, be_hbm, gi_hbm, wq_hbm, go_hbm, wh_hbm, bh_hbm,
     nf_hbm, ad_hbm, tl_hbm, sl_hbm, tot_ref, nf_ref, ad_ref, tl_ref, sl_ref,
     x_ref, par_ref, be_ref, gi_ref, go_ref, bh_ref, we, wq, wh, wep, whp, a1, a2, b2, tok, emb, nrm, qs, kv, mix,
     ht_s, ht_r, hx_s, hx_r, red_s, red_t,
     w_sem, o_sem, send, recv, fsend, frecv, sib_sem, halo_sem, rs_send, rs_recv, rt_send, rt_recv) = refs
    n_c = n_tm // 2
    me_t = lax.axis_index("tm")
    me_s = lax.axis_index("space")
    core = lax.rem(me_t, 2)
    chip = me_t // 2
    sibling = chip * 2 + 1 - core

    loads = [
        pltpu.make_async_copy(src, dst, w_sem.at[i])
        for i, (src, dst) in enumerate((
            (x_hbm, x_ref), (par_hbm, par_ref), (we_hbm, we), (wh_hbm, wh), (bh_hbm, bh_ref), (be_hbm, be_ref),
            (gi_hbm, gi_ref), (wq_hbm, wq), (go_hbm, go_ref)))
    ]
    for load in loads:
        load.start()
    barrier = pltpu.get_barrier_semaphore()
    for o in range(1, n_tm):
        pl.semaphore_signal(barrier, inc=1, device_id={"tm": lax.rem(me_t + o, n_tm)}, device_id_type=MESH)
    for o in range(1, n_s):
        pl.semaphore_signal(barrier, inc=1, device_id={"space": lax.rem(me_s + o, n_s)}, device_id_type=MESH)

    loads[0].wait()
    loads[1].wait()
    for t in range(4):
        for c in range(16):
            a1[pl.ds(t * 64 + c, 4, stride=16), :] = x_ref[t, :, c * 128 : c * 128 + 128]
    par_row = par_ref[0].astype(f32)
    spread_rows = jnp.where(iota((16, 128), 1) // 16 == iota((16, 128), 0) // 2, par_row, 0.0)
    pick = iota((128, 128), 0) % 16 == (iota((128, 128), 1) % 64) // 4
    par16 = dot(spread_rows.astype(bf16), jnp.where(pick, 1.0, 0.0).astype(bf16))
    par_full = jnp.concatenate([par16] * 16, axis=0)
    row = iota((256, 128), 0)
    lane = iota((256, 128), 1)
    site = (row // 64 + row // 16 + lane // 64 + lane) % 2
    frozen = site.astype(f32) == par_full
    u = a1[...]
    a2[...] = jnp.where(frozen, u, 0.0)
    rows_c = jnp.concatenate([a2[pl.ds(c, 16, stride=16), :] for c in range(16)], axis=0)
    r, l = iota((128, 128), 0), iota((128, 128), 1)
    q = jnp.where((r // 64 == l // 64) & ((r % 64) // 16 == l % 4) & (r % 16 == (l % 64) // 4), 1.0, 0.0).astype(bf16)
    spreadq = dot_nt(q, rows_c.astype(bf16))
    tok[me_t] = swap_blocks(spreadq, 8).astype(bf16)

    pl.semaphore_wait(barrier, n_tm - 1 + n_s - 1)
    own = pltpu.make_async_remote_copy(
        src_ref=tok.at[me_t], dst_ref=tok.at[me_t], send_sem=sib_sem.at[0], recv_sem=sib_sem.at[1],
        device_id={"tm": sibling}, device_id_type=MESH)
    sends = []
    for k in range(1, n_c):
        target = lax.rem(chip + k, n_c) * 2 + core
        sends.append(pltpu.make_async_remote_copy(
            src_ref=tok.at[me_t], dst_ref=tok.at[me_t], send_sem=send.at[k - 1], recv_sem=recv.at[k - 1],
            device_id={"tm": target}, device_id_type=MESH))
    for s in sends:
        s.start()
    own.start()
    forwards = []
    for k in range(1, n_c):
        block = lax.rem(chip - k + n_c, n_c) * 2 + core
        forwards.append(pltpu.make_async_remote_copy(
            src_ref=tok.at[block], dst_ref=tok.at[block], send_sem=fsend.at[k - 1], recv_sem=frecv.at[k - 1],
            device_id={"tm": sibling}, device_id_type=MESH))

    f, j = iota((256, 256), 0), iota((256, 256), 1)
    d = f // 32
    source = (f % 16) * 16 + ((f // 16) % 2) * 8 + (d // 4) * 4 + d % 4
    perm = jnp.where(j == source, 1.0, 0.0).astype(bf16)
    loads[2].wait()
    wep[...] = dot(perm, we[...]).astype(bf16)
    loads[3].wait()
    whp[:, :256] = dot_nt(wh[:, :256], perm).astype(bf16)
    whp[:, 256:] = dot_nt(wh[:, 256:], perm).astype(bf16)
    loads[4].wait()
    b_head = bh_ref[...].reshape(2, 256)
    b_hi = b_head.astype(bf16).astype(f32)
    b_mid = (b_head - b_hi).astype(bf16).astype(f32)
    b_lo = b_head - b_hi - b_mid
    parts = jnp.concatenate([b_hi, b_mid, b_lo, jnp.zeros((2, 256), f32)], axis=0)
    moved_b = dot_nt(parts.astype(bf16), perm)
    b_perm = moved_b[0:2] + moved_b[2:4] + moved_b[4:6]
    loads[5].wait()
    loads[6].wait()
    b_embed = be_ref[...].reshape(1, D)
    gain_in = gi_ref[...].reshape(1, D)
    loads[7].wait()
    loads[8].wait()

    for k in range(n_c):
        here = lax.rem(chip - k + n_c, n_c)
        if k == 0:
            own.wait_recv()
        else:
            if k == 1:
                sends[0].wait_recv()
                forwards[0].start()
            if k < n_c - 1:
                sends[k].wait_recv()
                forwards[k].start()
            forwards[k - 1].wait_recv()
        pair = tok[pl.ds(here * 2, 2)].reshape(2 * TOK, PATCH)
        embedded = dot(pair, wep[...]) + b_embed
        normed = layer_norm(embedded, gain_in).astype(bf16)
        if k == 0:
            emb[...] = embedded
            nrm[...] = normed
            mine = pl.ds(pl.multiple_of(core * TOK, TOK), TOK)
            qs[...] = dot(nrm[mine, :], wq[:, :D]).astype(bf16) * jnp.asarray(HS ** (-0.5), bf16)
        rows_at = pl.ds(pl.multiple_of(here * 2 * TOK, 2 * TOK), 2 * TOK)
        kv[rows_at, :] = dot(normed, wq[:, D:]).astype(bf16)

    if masked:
        nb, ksel = list_ref.shape
        mine_row = jnp.sum(jnp.where(iota((nb, ksel), 0) == me_t, list_ref[...], 0), axis=0, keepdims=True)
        key_block = iota((1, n_tm * TOK), 1) // TOK
        listed = key_block < 0
        for i in range(ksel):
            listed = listed | (key_block == mine_row[:, i : i + 1])
        bias = jnp.where(listed, 0.0, -1e30)
    low = iota((TOK, 128), 1) < HS

    def head_pair(h, carry):
        cols = pl.ds(pl.multiple_of(h * 128, 128), 128)
        vcols = pl.ds(pl.multiple_of(D + h * 128, 128), 128)
        qq = qs[:, cols]
        zero = jnp.zeros_like(qq)
        q2 = jnp.concatenate([jnp.where(low, qq, zero), jnp.where(low, zero, qq)], axis=0)
        s = dot_nt(q2, kv[:, cols])
        if masked:
            s = s + bias
        top = jnp.max(s, axis=-1, keepdims=True)
        ex = jnp.exp(s - top)
        total = jnp.sum(ex, axis=-1, keepdims=True)
        o = dot(ex.astype(bf16), kv[:, vcols]) / total
        mix[:, cols] = jnp.where(low, o[:TOK], o[TOK:])
        return carry

    lax.fori_loop(0, D // 128, head_pair, 0, unroll=True)

    hidden = emb[mine, :] + mix[...]
    normed_out = layer_norm(hidden, go_ref[...].reshape(1, D)).astype(bf16)
    raw = dot(normed_out, whp[...])
    scale_tok = jnp.tanh(raw[:, :256] + b_perm[0:1])
    shift_tok = raw[:, 256:] + b_perm[1:2]

    def to_lattice(values, ref):
        flipped = jnp.transpose(swap_blocks(values, 8))
        hi = flipped.astype(bf16)
        lo = (flipped - hi.astype(f32)).astype(bf16)
        ref[...] = dot(hi, q) + dot(lo, q)
        return jnp.concatenate([ref[pl.ds(i, 16, stride=16), :] for i in range(16)], axis=0)

    scale_log = to_lattice(scale_tok, a2)
    shift_val = to_lattice(shift_tok, b2)
    field = jnp.where(frozen, u, u * jnp.exp(scale_log) + shift_val)
    ht_s[...] = field[0:64].astype(bf16)
    hx_s[...] = jnp.concatenate([field[t * 64 : t * 64 + 16] for t in range(4)], axis=0).astype(bf16)
    halo_t = pltpu.make_async_remote_copy(
        src_ref=ht_s, dst_ref=ht_r, send_sem=halo_sem.at[0], recv_sem=halo_sem.at[1],
        device_id={"tm": lax.rem(me_t - 1 + n_tm, n_tm)}, device_id_type=MESH)
    halo_x = pltpu.make_async_remote_copy(
        src_ref=hx_s, dst_ref=hx_r, send_sem=halo_sem.at[2], recv_sem=halo_sem.at[3],
        device_id={"space": lax.rem(me_s - 1 + n_s, n_s)}, device_id_type=MESH)
    halo_t.start()
    halo_x.start()

    stores = []

    def put(ref, out, hbm):
        for t in range(4):
            for c in range(16):
                out[t, :, c * 128 : c * 128 + 128] = ref[pl.ds(t * 64 + c, 4, stride=16), :]
        store = pltpu.make_async_copy(out, hbm, o_sem.at[len(stores)])
        store.start()
        stores.append(store)

    a1[...] = field
    put(a1, nf_ref, nf_hbm)
    log_part = -0.5 * fold8(u * u) - fold8(jnp.where(frozen, 0.0, scale_log))
    ahead = pltpu.roll(field, 127, 1)
    wrapped = pltpu.roll(field, 63, 1)
    next_z = jnp.where(lane % 64 == 63, wrapped, ahead)
    half = pltpu.roll(field, 64, 1)
    up = pltpu.roll(half, 255, 0)
    up_wrap = pltpu.roll(half, 15, 0)
    next_y = jnp.where(lane < 64, half, jnp.where(row % 16 == 15, up_wrap, up))
    halo_t.wait_recv()
    next_t = jnp.concatenate([field[64:], ht_r[...].astype(f32)], axis=0)
    halo_x.wait_recv()
    hx = hx_r[...].astype(f32)
    pieces = []
    for t in range(4):
        pieces += [field[t * 64 + 16 : t * 64 + 64], hx[t * 16 : t * 16 + 16]]
    next_x = jnp.concatenate(pieces, axis=0)
    neighbours = next_t + next_x
    neighbours = neighbours + next_y
    neighbours = neighbours + next_z
    squared = field * field
    density = -2.0 * hopping * field * neighbours + squared + quartic * (squared - 1.0) * (squared - 1.0)

    red_s[me_s] = jnp.concatenate([log_part, fold8(density)], axis=0)
    s_sends = [
        pltpu.make_async_remote_copy(
            src_ref=red_s.at[me_s], dst_ref=red_s.at[me_s], send_sem=rs_send.at[o - 1], recv_sem=rs_recv.at[o - 1],
            device_id={"space": lax.rem(me_s + o, n_s)}, device_id_type=MESH)
        for o in range(1, n_s)
    ]
    for s in s_sends:
        s.start()
    a1[...] = density
    put(a1, ad_ref, ad_hbm)
    a2[...] = field * next_t
    put(a2, tl_ref, tl_hbm)
    for s in s_sends:
        s.wait_recv()
    red_t[me_t] = jnp.sum(red_s[...], axis=0)
    t_sends = [
        pltpu.make_async_remote_copy(
            src_ref=red_t.at[me_t], dst_ref=red_t.at[me_t], send_sem=rt_send.at[o - 1], recv_sem=rt_recv.at[o - 1],
            device_id={"tm": lax.rem(me_t + o, n_tm)}, device_id_type=MESH)
        for o in range(1, n_tm)
    ]
    for s in t_sends:
        s.start()
    b2[...] = field * next_x
    put(b2, sl_ref, sl_hbm)
    own.wait_send()
    for s in sends + forwards:
        s.wait_send()
    halo_t.wait_send()
    halo_x.wait_send()
    for s in s_sends:
        s.wait_send()
    for s in t_sends:
        s.wait_recv()
    whole = jnp.sum(red_t[...], axis=0)
    sites = n_s * n_tm * 256 * 128
    tot_ref[0] = jnp.sum(whole[0:8]) / sites - 0.5 * log_two_pi
    tot_ref[1] = jnp.sum(whole[8:16]) / sites
    for s in t_sends:
        s.wait_send()
    for s in stores:
        s.wait()


def write_out(*refs):
    sources, targets, sem = refs[:5], refs[5:10], refs[10]
    copies = [pltpu.make_async_copy(a, b, sem.at[i]) for i, (a, b) in enumerate(zip(sources, targets))]
    for c in copies:
        c.start()
    for c in copies:
        c.wait()


def shards(n_s, n_tm, lattice_field, parity, block_list, *weights):
    masked = block_list.shape[0] != block_list.shape[1]
    vm = pl.BlockSpec(memory_space=pltpu.VMEM)
    hbm = pl.BlockSpec(memory_space=pltpu.HBM)
    n_c = n_tm // 2
    grid_shape = jax.ShapeDtypeStruct(lattice_field.shape, f32)
    dma = pltpu.SemaphoreType.DMA
    call = pl.pallas_call(
        functools.partial(kernel, n_s, n_tm, masked),
        out_shape=(grid_shape,) * 4 + (jax.ShapeDtypeStruct((2,), f32),),
        in_specs=([vm] if masked else []) + [hbm] * 9,
        out_specs=(hbm,) * 4 + (pl.BlockSpec(memory_space=pltpu.SMEM),),
        scratch_shapes=[
            pltpu.VMEM(lattice_field.shape, f32),
            pltpu.VMEM(lattice_field.shape, f32),
            pltpu.VMEM(lattice_field.shape, f32),
            pltpu.VMEM(lattice_field.shape, f32),
            pltpu.VMEM(lattice_field.shape, f32),
            pltpu.VMEM(parity.shape, jnp.int32),
            pltpu.VMEM((D,), f32),
            pltpu.VMEM((D,), f32),
            pltpu.VMEM((D,), f32),
            pltpu.VMEM((2 * PATCH,), f32),
            pltpu.VMEM((PATCH, D), bf16),
            pltpu.VMEM((D, 3 * D), bf16),
            pltpu.VMEM((D, 2 * PATCH), bf16),
            pltpu.VMEM((PATCH, D), bf16),
            pltpu.VMEM((D, 2 * PATCH), bf16),
            pltpu.VMEM((256, 128), f32),
            pltpu.VMEM((256, 128), f32),
            pltpu.VMEM((256, 128), f32),
            pltpu.VMEM((n_tm, TOK, PATCH), bf16),
            pltpu.VMEM((2 * TOK, D), f32),
            pltpu.VMEM((2 * TOK, D), bf16),
            pltpu.VMEM((TOK, D), bf16),
            pltpu.VMEM((n_tm * TOK, 2 * D), bf16),
            pltpu.VMEM((TOK, D), f32),
            pltpu.VMEM((64, 128), bf16),
            pltpu.VMEM((64, 128), bf16),
            pltpu.VMEM((64, 128), bf16),
            pltpu.VMEM((64, 128), bf16),
            pltpu.VMEM((n_s, 16, 128), f32),
            pltpu.VMEM((n_tm, 16, 128), f32),
            dma((9,)),
            dma((4,)),
            dma((n_c - 1,)),
            dma((n_c - 1,)),
            dma((n_c - 1,)),
            dma((n_c - 1,)),
            dma((2,)),
            dma((4,)),
            dma((n_s - 1,)),
            dma((n_s - 1,)),
            dma((n_tm - 1,)),
            dma((n_tm - 1,)),
        ],
        compiler_params=pltpu.CompilerParams(
            collective_id=0, has_side_effects=True, vmem_limit_bytes=63 * 2**20
        ),
        cost_estimate=pl.CostEstimate(flops=5 * 10**9, bytes_accessed=6 * 10**6, transcendentals=2 * 10**6),
    )
    extra = (block_list,) if masked else ()
    results = call(*extra, lattice_field, parity, *weights)
    return pl.pallas_call(
        write_out,
        out_shape=[jax.ShapeDtypeStruct(r.shape, r.dtype) for r in results],
        in_specs=[vm] * 5,
        out_specs=[hbm] * 5,
        scratch_shapes=[dma((5,))],
        compiler_params=pltpu.CompilerParams(vmem_limit_bytes=63 * 2**20),
        cost_estimate=pl.CostEstimate(flops=0, bytes_accessed=2**20, transcendentals=0),
    )(*results)


def solution(mesh):
    n_s, n_tm = mesh.shape["space"], mesh.shape["tm"]
    split = P("tm", "space", None)
    return jax.shard_map(
        functools.partial(shards, n_s, n_tm),
        mesh=mesh,
        in_specs=(split, split) + (P(),) * 8,
        out_specs=(split,) * 4 + (P(),),
        check_vma=False,
    )
```

```python
import functools
import math

import jax
import jax.numpy as jnp
from jax import lax
from jax.experimental import pallas as pl
from jax.experimental.pallas import tpu as pltpu
from jax.sharding import PartitionSpec as P

D = 768
HS = 64
TOK = 128
PATCH = 256
hopping = 0.2
quartic = 0.5
epsilon = 1e-05
log_two_pi = math.log(2.0 * math.pi)
MESH = pl.DeviceIdType.MESH
f32 = jnp.float32
bf16 = jnp.bfloat16


def iota(shape, dim):
    return lax.broadcasted_iota(jnp.int32, shape, dim)


def dot(a, b):
    return jnp.dot(a, b, preferred_element_type=f32)


def dot_nt(a, b):
    return lax.dot_general(a, b, (((1,), (1,)), ((), ())), preferred_element_type=f32)


def layer_norm(values, gain_vec):
    centre = values - jnp.mean(values, axis=-1, keepdims=True)
    spread = jnp.mean(centre * centre, axis=-1, keepdims=True)
    return centre * lax.rsqrt(spread + epsilon) * gain_vec


def swap_blocks(m, n_a, n_b):
    rows = []
    for b in range(n_b):
        rows.append(
            jnp.concatenate(
                [m[a * 16 : a * 16 + 16, b * 32 : b * 32 + 32] for a in range(n_a)], axis=1
            )
        )
    return jnp.concatenate(rows, axis=0)


def fold8(a):
    return jnp.sum(a.reshape(a.shape[0] // 8, 8, 128), axis=0)


def kernel(n_s, n_tm, masked, *refs):
    if masked:
        list_ref, refs = refs[0], refs[1:]
    (x_hbm, par_hbm, we_hbm, be_hbm, gi_hbm, wq_hbm, go_hbm, wh_hbm, bh_hbm,
     nf_hbm, ad_hbm, tl_hbm, sl_hbm, tot_ref, nf_ref, ad_ref, tl_ref, sl_ref,
     x_ref, par_ref, be_ref, gi_ref, go_ref, bh_ref, we, wq, wh, wep, whp, a1, a2, b2, tok, emb, nrm, qs, kv, mix,
     ht_s, ht_r, hx_s, hx_r, red_s, red_t,
     w_sem, o_sem, send, recv, fsend, frecv, sib_sem, halo_sem, rs_send, rs_recv, rt_send, rt_recv) = refs
    n_c = n_tm // 2
    me_t = lax.axis_index("tm")
    me_s = lax.axis_index("space")
    core = lax.rem(me_t, 2)
    chip = me_t // 2
    sibling = chip * 2 + 1 - core

    loads = [
        pltpu.make_async_copy(src, dst, w_sem.at[i])
        for i, (src, dst) in enumerate((
            (x_hbm, x_ref), (par_hbm, par_ref), (we_hbm, we), (wh_hbm, wh), (bh_hbm, bh_ref), (be_hbm, be_ref),
            (gi_hbm, gi_ref), (wq_hbm, wq), (go_hbm, go_ref)))
    ]
    for load in loads:
        load.start()
    barrier = pltpu.get_barrier_semaphore()
    for o in range(1, n_tm):
        pl.semaphore_signal(barrier, inc=1, device_id={"tm": lax.rem(me_t + o, n_tm)}, device_id_type=MESH)
    for o in range(1, n_s):
        pl.semaphore_signal(barrier, inc=1, device_id={"space": lax.rem(me_s + o, n_s)}, device_id_type=MESH)

    loads[0].wait()
    loads[1].wait()
    for t in range(4):
        for c in range(16):
            a1[pl.ds(t * 64 + c, 4, stride=16), :] = x_ref[t, :, c * 128 : c * 128 + 128]
    par_row = par_ref[0].astype(f32)
    spread_rows = jnp.where(iota((16, 128), 1) // 16 == iota((16, 128), 0) // 2, par_row, 0.0)
    pick = iota((128, 128), 0) % 16 == (iota((128, 128), 1) % 64) // 4
    par16 = dot(spread_rows.astype(bf16), jnp.where(pick, 1.0, 0.0).astype(bf16))
    par_full = jnp.concatenate([par16] * 16, axis=0)
    row = iota((256, 128), 0)
    lane = iota((256, 128), 1)
    site = (row // 64 + row // 16 + lane // 64 + lane) % 2
    frozen = site.astype(f32) == par_full
    u = a1[...]
    a2[...] = jnp.where(frozen, u, 0.0)
    rows_c = jnp.concatenate([a2[pl.ds(c, 16, stride=16), :] for c in range(16)], axis=0)
    r, l = iota((128, 128), 0), iota((128, 128), 1)
    q = jnp.where((r // 64 == l // 64) & ((r % 64) // 16 == l % 4) & (r % 16 == (l % 64) // 4), 1.0, 0.0).astype(bf16)
    r64, l64 = iota((64, 128), 0), iota((64, 128), 1)
    q_pair = (r64 // 32 == l64 // 64) & ((r64 % 32) // 16 == (l64 % 4) // 2) & (r64 % 16 == (l64 % 64) // 4)
    spreadq = dot_nt(jnp.where(q_pair, 1.0, 0.0).astype(bf16), rows_c.astype(bf16))
    tok[me_t] = jnp.concatenate(
        [swap_blocks(spreadq, 4, 8), jnp.broadcast_to(par_row, (16, 128))], axis=0
    ).astype(bf16)

    pl.semaphore_wait(barrier, n_tm - 1 + n_s - 1)
    own = pltpu.make_async_remote_copy(
        src_ref=tok.at[me_t], dst_ref=tok.at[me_t], send_sem=sib_sem.at[0], recv_sem=sib_sem.at[1],
        device_id={"tm": sibling}, device_id_type=MESH)
    sends = []
    for k in range(1, n_c):
        target = lax.rem(chip + k, n_c) * 2 + core
        sends.append(pltpu.make_async_remote_copy(
            src_ref=tok.at[me_t], dst_ref=tok.at[me_t], send_sem=send.at[k - 1], recv_sem=recv.at[k - 1],
            device_id={"tm": target}, device_id_type=MESH))
    for s in sends:
        s.start()
    own.start()
    forwards = []
    for k in range(1, n_c):
        block = lax.rem(chip - k + n_c, n_c) * 2 + core
        forwards.append(pltpu.make_async_remote_copy(
            src_ref=tok.at[block], dst_ref=tok.at[block], send_sem=fsend.at[k - 1], recv_sem=frecv.at[k - 1],
            device_id={"tm": sibling}, device_id_type=MESH))

    f, j = iota((256, 256), 0), iota((256, 256), 1)
    d = f // 32
    column = (f % 16) * 16 + ((f // 16) % 2) * 8
    perm = jnp.where(j == column + d, 1.0, 0.0).astype(bf16)
    source = column + ((d // 2) % 2) * 4 + (d % 2) * 2 + d // 4
    perm_in = jnp.where(j == source, 1.0, 0.0).astype(bf16)
    loads[2].wait()
    wep[...] = dot(perm_in, we[...]).astype(bf16)
    loads[3].wait()
    whp[:, :256] = dot_nt(wh[:, :256], perm).astype(bf16)
    whp[:, 256:] = dot_nt(wh[:, 256:], perm).astype(bf16)
    loads[4].wait()
    b_head = bh_ref[...].reshape(2, 256)
    b_hi = b_head.astype(bf16).astype(f32)
    b_mid = (b_head - b_hi).astype(bf16).astype(f32)
    b_lo = b_head - b_hi - b_mid
    parts = jnp.concatenate([b_hi, b_mid, b_lo, jnp.zeros((2, 256), f32)], axis=0)
    moved_b = dot_nt(parts.astype(bf16), perm)
    b_perm = moved_b[0:2] + moved_b[2:4] + moved_b[4:6]
    loads[5].wait()
    loads[6].wait()
    b_embed = be_ref[...].reshape(1, D)
    gain_in = gi_ref[...].reshape(1, D)
    loads[7].wait()
    loads[8].wait()

    lane_t = iota((TOK, 128), 1)
    lane_bit = ((lane_t % 16) // 4 + lane_t % 4 + lane_t // 64) % 2
    lane_sign = jnp.where(lane_bit == 0, 1.0, -1.0)
    eye = iota((TOK, 128), 0) == lane_t

    def unpack(block):
        values = block[:TOK]
        bits = jnp.sum(jnp.where(eye, block[TOK : TOK + 1].astype(f32), 0.0), axis=1, keepdims=True)
        even = (1.0 - 2.0 * bits) * lane_sign > 0.0
        wide = values.astype(f32)
        return jnp.concatenate([jnp.where(even, wide, 0.0), jnp.where(even, 0.0, wide)], axis=1).astype(bf16)

    for k in range(n_c):
        here = lax.rem(chip - k + n_c, n_c)
        if k == 0:
            own.wait_recv()
        else:
            if k == 1:
                sends[0].wait_recv()
                forwards[0].start()
            if k < n_c - 1:
                sends[k].wait_recv()
                forwards[k].start()
            forwards[k - 1].wait_recv()
        both = [unpack(tok[here * 2]), unpack(tok[here * 2 + 1])]
        pair = jnp.concatenate(both, axis=0)
        embedded = dot(pair, wep[...]) + b_embed
        normed = layer_norm(embedded, gain_in).astype(bf16)
        if k == 0:
            emb[...] = embedded
            nrm[...] = normed
            mine = pl.ds(pl.multiple_of(core * TOK, TOK), TOK)
            qs[...] = dot(nrm[mine, :], wq[:, :D]).astype(bf16) * jnp.asarray(HS ** (-0.5), bf16)
        rows_at = pl.ds(pl.multiple_of(here * 2 * TOK, 2 * TOK), 2 * TOK)
        kv[rows_at, :] = dot(normed, wq[:, D:]).astype(bf16)

    if masked:
        nb, ksel = list_ref.shape
        mine_row = jnp.sum(jnp.where(iota((nb, ksel), 0) == me_t, list_ref[...], 0), axis=0, keepdims=True)
        key_block = iota((1, n_tm * TOK), 1) // TOK
        listed = key_block < 0
        for i in range(ksel):
            listed = listed | (key_block == mine_row[:, i : i + 1])
        bias = jnp.where(listed, 0.0, -1e30)
    low = iota((TOK, 128), 1) < HS

    def head_pair(h, carry):
        cols = pl.ds(pl.multiple_of(h * 128, 128), 128)
        vcols = pl.ds(pl.multiple_of(D + h * 128, 128), 128)
        qq = qs[:, cols]
        zero = jnp.zeros_like(qq)
        q2 = jnp.concatenate([jnp.where(low, qq, zero), jnp.where(low, zero, qq)], axis=0)
        s = dot_nt(q2, kv[:, cols])
        if masked:
            s = s + bias
        top = jnp.max(s, axis=-1, keepdims=True)
        ex = jnp.exp(s - top)
        total = jnp.sum(ex, axis=-1, keepdims=True)
        o = dot(ex.astype(bf16), kv[:, vcols]) / total
        mix[:, cols] = jnp.where(low, o[:TOK], o[TOK:])
        return carry

    lax.fori_loop(0, D // 128, head_pair, 0, unroll=True)

    hidden = emb[mine, :] + mix[...]
    normed_out = layer_norm(hidden, go_ref[...].reshape(1, D)).astype(bf16)
    raw = dot(normed_out, whp[...])
    scale_tok = jnp.tanh(raw[:, :256] + b_perm[0:1])
    shift_tok = raw[:, 256:] + b_perm[1:2]

    def to_lattice(values, ref):
        flipped = jnp.transpose(swap_blocks(values, 8, 8))
        hi = flipped.astype(bf16)
        lo = (flipped - hi.astype(f32)).astype(bf16)
        ref[...] = dot(hi, q) + dot(lo, q)
        return jnp.concatenate([ref[pl.ds(i, 16, stride=16), :] for i in range(16)], axis=0)

    scale_log = to_lattice(scale_tok, a2)
    shift_val = to_lattice(shift_tok, b2)
    field = jnp.where(frozen, u, u * jnp.exp(scale_log) + shift_val)
    ht_s[...] = field[0:64].astype(bf16)
    hx_s[...] = jnp.concatenate([field[t * 64 : t * 64 + 16] for t in range(4)], axis=0).astype(bf16)
    halo_t = pltpu.make_async_remote_copy(
        src_ref=ht_s, dst_ref=ht_r, send_sem=halo_sem.at[0], recv_sem=halo_sem.at[1],
        device_id={"tm": lax.rem(me_t - 1 + n_tm, n_tm)}, device_id_type=MESH)
    halo_x = pltpu.make_async_remote_copy(
        src_ref=hx_s, dst_ref=hx_r, send_sem=halo_sem.at[2], recv_sem=halo_sem.at[3],
        device_id={"space": lax.rem(me_s - 1 + n_s, n_s)}, device_id_type=MESH)
    halo_t.start()
    halo_x.start()

    stores = []

    def put(ref, out, hbm):
        for t in range(4):
            for c in range(16):
                out[t, :, c * 128 : c * 128 + 128] = ref[pl.ds(t * 64 + c, 4, stride=16), :]
        store = pltpu.make_async_copy(out, hbm, o_sem.at[len(stores)])
        store.start()
        stores.append(store)

    a1[...] = field
    put(a1, nf_ref, nf_hbm)
    log_part = -0.5 * fold8(u * u) - fold8(jnp.where(frozen, 0.0, scale_log))
    ahead = pltpu.roll(field, 127, 1)
    wrapped = pltpu.roll(field, 63, 1)
    next_z = jnp.where(lane % 64 == 63, wrapped, ahead)
    half = pltpu.roll(field, 64, 1)
    up = pltpu.roll(half, 255, 0)
    up_wrap = pltpu.roll(half, 15, 0)
    next_y = jnp.where(lane < 64, half, jnp.where(row % 16 == 15, up_wrap, up))
    halo_t.wait_recv()
    next_t = jnp.concatenate([field[64:], ht_r[...].astype(f32)], axis=0)
    halo_x.wait_recv()
    hx = hx_r[...].astype(f32)
    pieces = []
    for t in range(4):
        pieces += [field[t * 64 + 16 : t * 64 + 64], hx[t * 16 : t * 16 + 16]]
    next_x = jnp.concatenate(pieces, axis=0)
    neighbours = next_t + next_x
    neighbours = neighbours + next_y
    neighbours = neighbours + next_z
    squared = field * field
    density = -2.0 * hopping * field * neighbours + squared + quartic * (squared - 1.0) * (squared - 1.0)

    logs = jnp.sum(log_part, axis=0, keepdims=True)
    acts = jnp.sum(fold8(density), axis=0, keepdims=True)
    red_s[me_s] = jnp.where(
        iota((1, 128), 1) < 64, logs + pltpu.roll(logs, 64, 1), acts + pltpu.roll(acts, 64, 1)
    )
    s_sends = [
        pltpu.make_async_remote_copy(
            src_ref=red_s.at[me_s], dst_ref=red_s.at[me_s], send_sem=rs_send.at[o - 1], recv_sem=rs_recv.at[o - 1],
            device_id={"space": lax.rem(me_s + o, n_s)}, device_id_type=MESH)
        for o in range(1, n_s)
    ]
    for s in s_sends:
        s.start()
    a1[...] = density
    put(a1, ad_ref, ad_hbm)
    a2[...] = field * next_t
    put(a2, tl_ref, tl_hbm)
    for s in s_sends:
        s.wait_recv()
    red_t[me_t] = jnp.sum(red_s[...], axis=0)
    t_sends = [
        pltpu.make_async_remote_copy(
            src_ref=red_t.at[me_t], dst_ref=red_t.at[me_t], send_sem=rt_send.at[o - 1], recv_sem=rt_recv.at[o - 1],
            device_id={"tm": lax.rem(me_t + o, n_tm)}, device_id_type=MESH)
        for o in range(1, n_tm)
    ]
    for s in t_sends:
        s.start()
    b2[...] = field * next_x
    put(b2, sl_ref, sl_hbm)
    own.wait_send()
    for s in sends + forwards:
        s.wait_send()
    halo_t.wait_send()
    halo_x.wait_send()
    for s in s_sends:
        s.wait_send()
    for s in t_sends:
        s.wait_recv()
    whole = jnp.sum(red_t[...], axis=0)
    first = iota((1, 128), 1) < 64
    sites = n_s * n_tm * 256 * 128
    tot_ref[0] = jnp.sum(jnp.where(first, whole, 0.0)) / sites - 0.5 * log_two_pi
    tot_ref[1] = jnp.sum(jnp.where(first, 0.0, whole)) / sites
    for s in t_sends:
        s.wait_send()
    for s in stores:
        s.wait()


def write_out(*refs):
    sources, targets, sem = refs[:5], refs[5:10], refs[10]
    copies = [pltpu.make_async_copy(a, b, sem.at[i]) for i, (a, b) in enumerate(zip(sources, targets))]
    for c in copies:
        c.start()
    for c in copies:
        c.wait()


def shards(n_s, n_tm, lattice_field, parity, block_list, *weights):
    masked = block_list.shape[0] != block_list.shape[1]
    vm = pl.BlockSpec(memory_space=pltpu.VMEM)
    hbm = pl.BlockSpec(memory_space=pltpu.HBM)
    n_c = n_tm // 2
    grid_shape = jax.ShapeDtypeStruct(lattice_field.shape, f32)
    dma = pltpu.SemaphoreType.DMA
    call = pl.pallas_call(
        functools.partial(kernel, n_s, n_tm, masked),
        out_shape=(grid_shape,) * 4 + (jax.ShapeDtypeStruct((2,), f32),),
        in_specs=([vm] if masked else []) + [hbm] * 9,
        out_specs=(hbm,) * 4 + (pl.BlockSpec(memory_space=pltpu.SMEM),),
        scratch_shapes=[
            pltpu.VMEM(lattice_field.shape, f32),
            pltpu.VMEM(lattice_field.shape, f32),
            pltpu.VMEM(lattice_field.shape, f32),
            pltpu.VMEM(lattice_field.shape, f32),
            pltpu.VMEM(lattice_field.shape, f32),
            pltpu.VMEM(parity.shape, jnp.int32),
            pltpu.VMEM((D,), f32),
            pltpu.VMEM((D,), f32),
            pltpu.VMEM((D,), f32),
            pltpu.VMEM((2 * PATCH,), f32),
            pltpu.VMEM((PATCH, D), bf16),
            pltpu.VMEM((D, 3 * D), bf16),
            pltpu.VMEM((D, 2 * PATCH), bf16),
            pltpu.VMEM((PATCH, D), bf16),
            pltpu.VMEM((D, 2 * PATCH), bf16),
            pltpu.VMEM((256, 128), f32),
            pltpu.VMEM((256, 128), f32),
            pltpu.VMEM((256, 128), f32),
            pltpu.VMEM((n_tm, TOK + 16, 128), bf16),
            pltpu.VMEM((2 * TOK, D), f32),
            pltpu.VMEM((2 * TOK, D), bf16),
            pltpu.VMEM((TOK, D), bf16),
            pltpu.VMEM((n_tm * TOK, 2 * D), bf16),
            pltpu.VMEM((TOK, D), f32),
            pltpu.VMEM((64, 128), bf16),
            pltpu.VMEM((64, 128), bf16),
            pltpu.VMEM((64, 128), bf16),
            pltpu.VMEM((64, 128), bf16),
            pltpu.VMEM((n_s, 1, 128), f32),
            pltpu.VMEM((n_tm, 1, 128), f32),
            dma((9,)),
            dma((4,)),
            dma((n_c - 1,)),
            dma((n_c - 1,)),
            dma((n_c - 1,)),
            dma((n_c - 1,)),
            dma((2,)),
            dma((4,)),
            dma((n_s - 1,)),
            dma((n_s - 1,)),
            dma((n_tm - 1,)),
            dma((n_tm - 1,)),
        ],
        compiler_params=pltpu.CompilerParams(
            collective_id=0, has_side_effects=True, vmem_limit_bytes=63 * 2**20
        ),
        cost_estimate=pl.CostEstimate(flops=5 * 10**9, bytes_accessed=6 * 10**6, transcendentals=2 * 10**6),
    )
    extra = (block_list,) if masked else ()
    results = call(*extra, lattice_field, parity, *weights)
    return pl.pallas_call(
        write_out,
        out_shape=[jax.ShapeDtypeStruct(r.shape, r.dtype) for r in results],
        in_specs=[vm] * 5,
        out_specs=[hbm] * 5,
        scratch_shapes=[dma((5,))],
        compiler_params=pltpu.CompilerParams(vmem_limit_bytes=63 * 2**20),
        cost_estimate=pl.CostEstimate(flops=0, bytes_accessed=2**20, transcendentals=0),
    )(*results)


def solution(mesh):
    n_s, n_tm = mesh.shape["space"], mesh.shape["tm"]
    split = P("tm", "space", None)
    return jax.shard_map(
        functools.partial(shards, n_s, n_tm),
        mesh=mesh,
        in_specs=(split, split) + (P(),) * 8,
        out_specs=(split,) * 4 + (P(),),
        check_vma=False,
    )
```
